32 devices in a mesh: row: 8 (over z, x), col: 4 (over y, core).
Axes of the slice: x: 2, y: 2, z: 4, core: 2. Of those that a mesh axis runs over, the one named last changes fastest.
Arguments:
- a_vals: float32 [8, 4, 448, 4096], P('row', 'col'), may hold values from -0.1875 to 0.1875
- a_row: int32 [8, 4, 448], P('row', 'col'), may hold values from 0 to 31
- a_col: int32 [8, 4, 448], P('row', 'col'), may hold values from 0 to 63
- a_slot: int32 [8, 4, 3, 448], P('row', 'col'), may hold values from 0 to 5
- a_count: int32 [8, 4], P('row', 'col'), may hold values from 1 to 448, as said below
- p_vals: float32 [256, 3, 4096], P(('row', 'col')), may hold values from -0.75 to 0.75
- p_owner: int32 [256, 3], P(('row', 'col')), may hold values from 0 to 7, all different within a row; in each aligned block of 8 rows (0 to 7, 8 to 15, ...) at most 4 rows name the same one
- p_sub: int32 [256, 3], P(('row', 'col')), may hold values from 0 to 3
- ap_cslot: int32 [256, 3, 6], P(('row', 'col')), may hold values from 0 to 26
Outputs:
- coarse: float32 [32, 27, 4096], P(('row', 'col'))
The draws below stay inside these ranges and needn't reach their ends.
Inputs may be any that keep to these rules, and one draw needn't show every extreme that they name: `a_count`: at least one device holds exactly 448 listed blocks. `p_owner`: the 3 entries of a fine block row differ; among the rows of one device each row group is named at most 4 times.
All inputs are finite; a program needn't handle non-finite values.
Results may differ from the reference program's by a relative error of at most 0.0001.
Values sent between devices are 32-bit elements; how exact they have to be, the bound alone decides.
A program may use at most 128 MiB of HBM per device.

```python
import math
import jax
import jax.numpy as jnp
import numpy as np
from jax import lax

BLOCK = 64
TILE = 4096
RPD = 8
TP = 3
TAP = 6
TC = 27
TA = 448
RG = 32
CG = 64
NB = 256
CRG = 4
NC = 32
CAPR = 4
N_ROW = 8
N_COL = 4


def draw_a_count(key, part):
    key_levels, key_pick, key_jitter = jax.random.split(key, 3)
    devices_all = N_ROW * N_COL
    levels = jax.random.randint(key_levels, (devices_all,), 1, 5)
    weights = levels * levels
    chosen = jax.random.randint(key_pick, (), 0, devices_all)
    marked = jnp.arange(devices_all) == chosen
    weights = jnp.where(marked, 16, weights)
    jitter = jax.random.randint(key_jitter, (devices_all,), 0, TA // 32 + 1)
    jitter = jnp.where(marked, 0, jitter)
    counts = jnp.maximum(TA * weights // 16 - jitter, 1)
    return counts.reshape(N_ROW, N_COL).astype(jnp.int32)


def plant(drawn, own_key, smallest, high):
    place = [jax.random.randint(jax.random.fold_in(own_key, axis), (), 0, length) for axis, length in enumerate(drawn.shape)]
    widest = drawn.shape.index(max(drawn.shape))
    next_to = place[:widest] + [(place[widest] + 1) % drawn.shape[widest]] + place[widest + 1:]
    return drawn.at[tuple(place)].set(smallest).at[tuple(next_to)].set(high)


def block_levels(key, shape, cuts, smallest, top_value):
    factor_of, own = 1.0, jax.random.fold_in(key, 6)
    for dim, shards_of in cuts:
        draws = jnp.exp(jax.random.uniform(jax.random.fold_in(own, dim), (shards_of,), jnp.float32, smallest / len(cuts), top_value / len(cuts)))
        factor_of = factor_of * jnp.repeat(draws, shape[dim] // shards_of).reshape([-1 if axis == dim else 1 for axis in range(len(shape))])
    return factor_of


def deal_out(stream_key, own, number, rows, number_of, top, most, skew):
    order = jax.random.permutation(stream_key, number_of)
    heavy_load, common = shares(number_of, rows * top, most, skew, True), shares(number_of, rows * top, most, skew, False)
    places = jnp.arange(number_of)

    def named(lengths, offset_by):
        used = int((lengths > 0).sum())
        fixed = max(1, used // 4)
        passed = fixed + (places - fixed + offset_by * (used - fixed)) % max(1, number_of - fixed)
        return jnp.zeros((number_of,), jnp.int32).at[order[jnp.where(places < fixed, places, passed)]].set(jnp.asarray(lengths, jnp.int32))

    lengths = jnp.where(number % 4 == 0, named(heavy_load, number // 4), named(common, number - number // 4 - 1))
    mixed = jax.random.permutation(jax.random.fold_in(own, 3), number_of)
    donor, taker = mixed[0:number_of // 2 * 2:2], mixed[1:number_of // 2 * 2:2]
    margin = jnp.minimum(lengths[donor] - 1, most - lengths[taker]) // 2
    margin = jnp.where((donor == order[0]) | (taker == order[0]) | (lengths[taker] == 0), 0, jnp.maximum(margin, 0))
    passed = jax.random.randint(jax.random.fold_in(own, 4), (number_of // 2,), 0, 1 << 20) % (margin + 1)
    lengths = lengths.at[donor].add(-passed).at[taker].add(passed)
    labels = jnp.searchsorted(jnp.cumsum(lengths), jnp.arange(rows * top), side="right").astype(jnp.int32)
    listing = labels.reshape(top, rows).T
    listing = listing[jax.random.permutation(jax.random.fold_in(own, 1), rows)]
    offset_by = jax.random.randint(jax.random.fold_in(own, 2), (rows, 1), 0, top)
    return jnp.take_along_axis(listing, (jnp.arange(top)[None, :] + offset_by) % top, axis=1)


def shares(amount, total, most, slope, full):
    portions = [(1 << 20) // math.isqrt(rank ** slope) + 1 for rank in range(1, amount + 1)]
    largest = most if full else min(most, max(-(-total // amount), total * portions[0] // sum(portions)))
    least = 1 if total - largest >= amount - 1 else 0
    given, surplus = [largest] + [least] * (amount - 1), total - largest - least * (amount - 1)
    while surplus > 0:
        candidates = [i for i in range(1, amount) if given[i] < largest] or [i for i in range(1, amount) if given[i] < most]
        mass, budget = sum([portions[i] for i in candidates]), surplus
        for i in candidates:
            more = min(most - given[i], max(1, budget * portions[i] // mass), surplus)
            given[i] = given[i] + more
            surplus = surplus - more
    return np.array(given)


def centred(own_key, dims, scale, reach, cuts=(), kind=jnp.bfloat16):
    result = scale * jax.random.normal(own_key, dims, jnp.float32)
    if cuts:
        result = result * block_levels(own_key, dims, cuts, -0.22, 0.18)
    return jnp.clip(result, -reach, reach).astype(kind)


def setup_inputs(seed: int = 0) -> dict:
    key_of = jax.random.split(jax.random.key(seed), 10)
    a_vals = centred(key_of[0], (N_ROW, N_COL, TA, TILE), (BLOCK * 16) ** -0.5, 0.1875, ((0, 8), (1, 4)), jnp.float32)
    a_row = plant(jax.random.randint(key_of[1], (N_ROW, N_COL, TA), 0, RG), jax.random.fold_in(key_of[1], 1), 0, RG - 1).astype(jnp.int32)
    a_col = plant(jax.random.randint(key_of[2], (N_ROW, N_COL, TA), 0, CG), jax.random.fold_in(key_of[2], 1), 0, CG - 1).astype(jnp.int32)
    a_slot = plant(jax.random.randint(key_of[3], (N_ROW, N_COL, TP, TA), 0, TAP), jax.random.fold_in(key_of[3], 1), 0, TAP - 1).astype(jnp.int32)
    a_count = draw_a_count(jax.random.fold_in(key_of[9], 71), 0)
    p_vals = centred(key_of[5], (NB, TP, TILE), BLOCK ** -0.5, 0.75, ((0, 32),), jnp.float32)
    p_owner_keys = jax.random.split(jax.random.fold_in(key_of[6], 1), NB // RPD)
    p_owner_turns = jax.random.permutation(jax.random.fold_in(key_of[6], 3), NB // RPD)
    p_owner = jax.vmap(lambda own, number: deal_out(jax.random.fold_in(key_of[6], 2), own, number, RPD, N_ROW, TP, CAPR, 1))(p_owner_keys, p_owner_turns).reshape((NB, TP))
    p_sub = plant(jax.random.randint(key_of[7], (NB, TP), 0, CRG), jax.random.fold_in(key_of[7], 1), 0, CRG - 1).astype(jnp.int32)
    ap_cslot = plant(jax.random.randint(key_of[8], (NB, TP, TAP), 0, TC), jax.random.fold_in(key_of[8], 1), 0, TC - 1).astype(jnp.int32)
    return dict(a_vals=a_vals, a_row=a_row, a_col=a_col, a_slot=a_slot, a_count=a_count, p_vals=p_vals, p_owner=p_owner, p_sub=p_sub, ap_cslot=ap_cslot)


highest = lax.Precision.HIGHEST


def reference(a_vals, a_row, a_col, a_slot, a_count, p_vals, p_owner, p_sub, ap_cslot):
    devices_all = N_ROW * N_COL
    tiles_flat = a_vals.reshape(devices_all, TA, BLOCK, BLOCK)
    rows_flat = a_row.reshape(devices_all, TA).astype(jnp.int32)
    cols_flat = a_col.reshape(devices_all, TA).astype(jnp.int32)
    slots_flat = a_slot.reshape(devices_all, TP, TA).astype(jnp.int32)
    counts_flat = a_count.reshape(devices_all).astype(jnp.int32)
    prolong = p_vals.reshape(NB, TP, BLOCK, BLOCK)

    def add_device(device, product_sum):
        row_group = device // N_COL
        col_group = device % N_COL
        matrix_tiles = lax.dynamic_index_in_dim(tiles_flat, device, 0, False)
        tile_rows = lax.dynamic_index_in_dim(rows_flat, device, 0, False)
        tile_cols = lax.dynamic_index_in_dim(cols_flat, device, 0, False)
        tile_slots = lax.dynamic_index_in_dim(slots_flat, device, 0, False)
        tile_count = lax.dynamic_index_in_dim(counts_flat, device, 0, False)
        fine_col = (tile_cols // RPD) * RG + col_group * RPD + tile_cols % RPD
        right_tiles = jnp.take(prolong, fine_col.astype(jnp.int32), axis=0)
        products = jnp.einsum("tij,tsjk->tsik", matrix_tiles, right_tiles, precision=highest)
        is_live = jnp.arange(TA, dtype=jnp.int32) < tile_count
        products = jnp.where(is_live[:, None, None, None], products, jnp.zeros_like(products))
        target = (row_group * RG + tile_rows)[:, None] * TAP + tile_slots.T
        return product_sum.at[target.reshape(-1).astype(jnp.int32)].add(products.reshape(TA * TP, TILE))

    product_sum = lax.fori_loop(0, devices_all, add_device, jnp.zeros((NB * TAP, TILE), jnp.float32))
    ap_tiles = product_sum.reshape(NB, TAP, BLOCK, BLOCK)
    coarse_row = p_owner.astype(jnp.int32) * CRG + p_sub.astype(jnp.int32)
    cslots = ap_cslot.astype(jnp.int32)
    coarse_sum = jnp.zeros((NC * TC, TILE), jnp.float32)
    for branch in range(TP):
        left_tiles = prolong[:, branch]
        contribs = jnp.einsum("ijk,iqjl->iqkl", left_tiles, ap_tiles, precision=highest)
        target = coarse_row[:, branch][:, None] * TC + cslots[:, branch, :]
        coarse_sum = coarse_sum.at[target.reshape(-1).astype(jnp.int32)].add(contribs.reshape(NB * TAP, TILE))
    return coarse_sum.reshape(NC, TC, TILE)
```

```python
import functools

import jax
import jax.numpy as jnp
from jax import lax
from jax.experimental import pallas as pl
from jax.experimental.pallas import tpu as pltpu
from jax.sharding import PartitionSpec as P

BLOCK = 64
HALF = 32
LANES = 128
CPD = 1
TAP = 6
TC = 27
UNROLL = 4

VMEM = pl.BlockSpec(memory_space=pltpu.VMEM)
SMEM = pl.BlockSpec(memory_space=pltpu.SMEM)


def low_lanes(rows):
    return lax.broadcasted_iota(jnp.int32, (rows, LANES), 1) < BLOCK


def halves(value):
    high = value.astype(jnp.bfloat16)
    return high, (value - high.astype(jnp.float32)).astype(jnp.bfloat16)


def side_by_side(first, second):
    low = low_lanes(HALF)
    even = jnp.where(low, first, pltpu.roll(second, BLOCK, 1))
    odd = jnp.where(low, pltpu.roll(first, BLOCK, 1), second)
    return even, odd


def alone(first):
    low = low_lanes(HALF)
    return jnp.where(low, first, 0.0), jnp.where(low, pltpu.roll(first, BLOCK, 1), 0.0)


def ap_kernel(columns, targets, count_ref, col_ref, target_ref, a_ref, panel_ref, out_ref, weights, total, rows_ref):
    capacity = a_ref.shape[0]

    def weight_step(k, carry):
        first = panel_ref[3 * k]
        second = panel_ref[3 * k + 1]
        third = panel_ref[3 * k + 2]
        even, odd = side_by_side(first, second)
        rows_ref[0, pl.ds(0, HALF, stride=2), :] = even
        rows_ref[0, pl.ds(1, HALF, stride=2), :] = odd
        even, odd = alone(third)
        rows_ref[1, pl.ds(0, HALF, stride=2), :] = even
        rows_ref[1, pl.ds(1, HALF, stride=2), :] = odd
        high, rest = halves(jnp.concatenate([rows_ref[0], rows_ref[1]], axis=1))
        weights[k, 0:64, :] = high
        weights[k, 64:128, :] = high
        weights[k, 128:192, :] = rest
        weights[k, 192:256, :] = rest
        return carry

    lax.fori_loop(0, columns, weight_step, 0)

    def zero_step(i, carry):
        total[i] = jnp.zeros((BLOCK, LANES), jnp.float32)
        return carry

    lax.fori_loop(0, targets + 1, zero_step, 0)
    low_a = low_lanes(HALF)
    low = low_lanes(BLOCK)

    def block_step(step, carry):
        results = []
        for u in range(UNROLL):
            t = step * UNROLL + u
            value = a_ref[t]
            rounded = value.astype(jnp.bfloat16).astype(jnp.float32)
            rest = value - rounded
            even = jnp.where(low_a, rounded, pltpu.roll(rest, BLOCK, 1))
            odd = jnp.where(low_a, pltpu.roll(rounded, BLOCK, 1), rest)
            left = jnp.concatenate([even, odd], axis=0).astype(jnp.bfloat16)
            left = jnp.concatenate([left, left], axis=1)
            results.append(jnp.dot(left, weights[col_ref[t]], preferred_element_type=jnp.float32))
        for u in range(UNROLL):
            t = step * UNROLL + u
            pair = results[u][:, 0:LANES]
            total[target_ref[t]] += jnp.where(low, pair, 0.0)
            total[target_ref[capacity + t]] += jnp.where(low, 0.0, pair)
            total[target_ref[2 * capacity + t]] += results[u][:, LANES:2 * LANES]
        return carry

    lax.fori_loop(0, (count_ref[0] + UNROLL - 1) // UNROLL, block_step, 0)

    def out_step(i, carry):
        value = total[i]
        value = value + pltpu.roll(value, BLOCK, 1)
        out_ref[i] = jnp.where(low_a, value[0:HALF], value[HALF:BLOCK])
        return carry

    lax.fori_loop(0, targets, out_step, 0)


def coarse_kernel(rows, place_ref, ap_ref, p_ref, out_ref, result_ref):
    low = low_lanes(HALF)

    def row_step(i, carry):
        rights = []
        for pair in range(TAP // 2):
            even, odd = side_by_side(ap_ref[TAP * i + 2 * pair], ap_ref[TAP * i + 2 * pair + 1])
            rights.append(jnp.concatenate([even, odd], axis=0))
        high, rest = halves(jnp.concatenate(rights, axis=1))
        right = jnp.concatenate([high, rest, high, rest], axis=0)
        left_pair = jnp.concatenate(side_by_side(p_ref[3 * i], p_ref[3 * i + 1]), axis=0)
        left_one = jnp.concatenate(alone(p_ref[3 * i + 2]), axis=0)
        high, rest = halves(jnp.concatenate([left_pair, left_one], axis=1))
        left = jnp.concatenate([high, high, rest, rest], axis=0)
        result = lax.dot_general(
            left, right, (((0,), (0,)), ((), ())), preferred_element_type=jnp.float32
        )
        for pair in range(TAP // 2):
            result_ref[pair] = result[:, pair * LANES:(pair + 1) * LANES]
        for s in range(3):
            base = place_ref[3 * i + s] * TAP
            for pair in range(TAP // 2):
                even = result_ref[pair, pl.ds(s * BLOCK, HALF, stride=2), :]
                odd = result_ref[pair, pl.ds(s * BLOCK + 1, HALF, stride=2), :]
                out_ref[base + 2 * pair] = jnp.where(low, even, pltpu.roll(odd, BLOCK, 1))
                out_ref[base + 2 * pair + 1] = jnp.where(low, pltpu.roll(even, BLOCK, 1), odd)
        return carry

    lax.fori_loop(0, rows, row_step, 0)


def add_kernel(target_ref, in_ref, out_ref):
    out_ref[...] = jnp.zeros_like(out_ref)

    def step(e, carry):
        target = target_ref[e]

        @pl.when(target >= 0)
        def _():
            out_ref[target] += in_ref[e]

        return carry

    lax.fori_loop(0, in_ref.shape[0], step, 0)


def on_device(a_vals, a_row, a_col, a_slot, a_count, p_vals, p_owner, p_sub, ap_cslot):
    row_devices = lax.axis_size("row")
    col_devices = lax.axis_size("col")
    capacity = a_vals.shape[2]
    rows_dev = p_vals.shape[0]
    branches = p_vals.shape[1]
    group_rows = rows_dev * col_devices
    group_coarse = CPD * col_devices
    columns = rows_dev * row_devices
    targets = group_rows * TAP
    per_peer = max(2, 3 * rows_dev * branches // (2 * row_devices))
    item_count = rows_dev * branches
    slots_total = row_devices * per_peer
    f32 = jnp.float32

    p_local = p_vals.reshape(item_count, HALF, LANES)
    panel = lax.all_gather(p_local, "row", axis=0, tiled=True)

    a_blocks = a_vals.reshape(capacity, HALF, LANES)
    count = a_count.reshape(1)
    col_index = a_col.reshape(capacity)
    live = jnp.arange(capacity, dtype=jnp.int32) < count
    target = a_row.reshape(1, capacity) * TAP + a_slot.reshape(branches, capacity)
    target = jnp.where(live[None, :], target, targets).reshape(branches * capacity)

    owners = p_owner.reshape(item_count)
    serial = jnp.arange(item_count, dtype=jnp.int32)
    earlier = (owners[:, None] == owners[None, :]) & (serial[None, :] < serial[:, None])
    placed = owners * per_peer + jnp.sum(earlier.astype(jnp.int32), axis=1)
    metadata = p_sub.reshape(item_count, 1) * TC + ap_cslot.reshape(item_count, TAP)
    meta_send = jnp.full((slots_total, TAP), -1.0, f32).at[placed].set(metadata.astype(f32))
    meta_in = lax.all_to_all(meta_send, "row", split_axis=0, concat_axis=0, tiled=True)
    arrived_target = meta_in.astype(jnp.int32).reshape(slots_total * TAP)

    partial_ap = pl.pallas_call(
        functools.partial(ap_kernel, columns, targets),
        out_shape=jax.ShapeDtypeStruct((targets, HALF, LANES), f32),
        in_specs=[SMEM, SMEM, SMEM, VMEM, VMEM],
        out_specs=VMEM,
        scratch_shapes=[
            pltpu.VMEM((columns, 4 * BLOCK, 2 * LANES), jnp.bfloat16),
            pltpu.VMEM((targets + 1, BLOCK, LANES), f32),
            pltpu.VMEM((2, BLOCK, LANES), f32),
        ],
        compiler_params=pltpu.CompilerParams(vmem_limit_bytes=60 << 20),
        cost_estimate=pl.CostEstimate(
            flops=capacity * 2 * 64 * 256 * 256, bytes_accessed=14 << 20, transcendentals=0
        ),
        name="ap",
    )(count, col_index, target, a_blocks, panel)

    ap_rows = lax.psum_scatter(partial_ap, "col", scatter_dimension=0, tiled=True)

    outgoing = pl.pallas_call(
        functools.partial(coarse_kernel, rows_dev),
        out_shape=jax.ShapeDtypeStruct((slots_total * TAP, HALF, LANES), f32),
        in_specs=[SMEM, VMEM, VMEM],
        out_specs=VMEM,
        scratch_shapes=[pltpu.VMEM((TAP // 2, 2 * LANES, LANES), f32)],
        compiler_params=pltpu.CompilerParams(vmem_limit_bytes=32 << 20),
        name="coarse",
    )(placed, ap_rows, p_local)

    incoming = lax.all_to_all(outgoing, "row", split_axis=0, concat_axis=0, tiled=True)

    coarse_part = pl.pallas_call(
        add_kernel,
        out_shape=jax.ShapeDtypeStruct((group_coarse * TC, HALF, LANES), f32),
        in_specs=[SMEM, VMEM],
        out_specs=VMEM,
        compiler_params=pltpu.CompilerParams(vmem_limit_bytes=32 << 20),
        name="gather_coarse",
    )(arrived_target, incoming)

    coarse = lax.psum_scatter(coarse_part, "col", scatter_dimension=0, tiled=True)
    return coarse.reshape(CPD, TC, BLOCK * BLOCK)


def solution(mesh):
    placed = (
        P("row", "col", None, None),
        P("row", "col", None),
        P("row", "col", None),
        P("row", "col", None, None),
        P("row", "col"),
        P(("row", "col"), None, None),
        P(("row", "col"), None),
        P(("row", "col"), None),
        P(("row", "col"), None, None),
    )
    return jax.shard_map(
        on_device,
        mesh=mesh,
        in_specs=placed,
        out_specs=P(("row", "col"), None, None),
        check_vma=False,
    )
```

```python
import functools

import jax
import jax.numpy as jnp
from jax import lax
from jax.experimental import pallas as pl
from jax.experimental.pallas import tpu as pltpu
from jax.sharding import PartitionSpec as P

BLOCK = 64
HALF = 32
LANES = 128
CPD = 1
TAP = 6
TC = 27
CHUNK = 4

VMEM = pl.BlockSpec(memory_space=pltpu.VMEM)
SMEM = pl.BlockSpec(memory_space=pltpu.SMEM)


def low_lanes(rows):
    return lax.broadcasted_iota(jnp.int32, (rows, LANES), 1) < BLOCK


def halves(value):
    high = value.astype(jnp.bfloat16)
    return high, (value - high.astype(jnp.float32)).astype(jnp.bfloat16)


def side_by_side(first, second):
    low = low_lanes(HALF)
    even = jnp.where(low, first, pltpu.roll(second, BLOCK, 1))
    odd = jnp.where(low, pltpu.roll(first, BLOCK, 1), second)
    return even, odd


def alone(first):
    low = low_lanes(HALF)
    return jnp.where(low, first, 0.0), jnp.where(low, pltpu.roll(first, BLOCK, 1), 0.0)


def plan_kernel(columns, dump, count_ref, col_ref, target_ref, order_ref, place_ref, chunk_ref, total_ref, fill):
    capacity = col_ref.shape[0]
    slots = order_ref.shape[0]
    count = count_ref[0]

    def clear_column(k, carry):
        fill[k] = 0
        return carry

    lax.fori_loop(0, columns, clear_column, 0)

    def clear_slot(i, carry):
        order_ref[i] = 0
        for s in range(3):
            place_ref[s * (slots + CHUNK) + i] = dump
        return carry

    lax.fori_loop(0, slots, clear_slot, 0)
    for i in range(CHUNK):
        for s in range(3):
            place_ref[s * (slots + CHUNK) + slots + i] = dump

    def clear_chunk(i, carry):
        chunk_ref[i] = 0
        return carry

    lax.fori_loop(0, slots // CHUNK, clear_chunk, 0)

    def tally(t, carry):
        fill[col_ref[t]] += 1
        return carry

    lax.fori_loop(0, count, tally, 0)

    def open_column(k, first):
        chunks = (fill[k] + CHUNK - 1) // CHUNK
        fill[k] = first * CHUNK

        def mark(j, carry):
            chunk_ref[first + j] = k
            return carry

        lax.fori_loop(0, chunks, mark, 0)
        return first + chunks

    total_ref[0] = lax.fori_loop(0, columns, open_column, 0)

    def put(t, carry):
        k = col_ref[t]
        at = fill[k]
        fill[k] = at + 1
        order_ref[at] = t
        for s in range(3):
            place_ref[s * (slots + CHUNK) + CHUNK + at] = target_ref[s * capacity + t]
        return carry

    lax.fori_loop(0, count, put, 0)


def ap_kernel(columns, targets, chunks_ref, order_ref, place_ref, chunk_ref, a_ref, panel_ref, out_ref, weights, total, rows_ref, first_ref, second_ref):
    slots = order_ref.shape[0]

    def weight_step(k, carry):
        first = panel_ref[3 * k]
        second = panel_ref[3 * k + 1]
        third = panel_ref[3 * k + 2]
        even, odd = side_by_side(first, second)
        rows_ref[0, pl.ds(0, HALF, stride=2), :] = even
        rows_ref[0, pl.ds(1, HALF, stride=2), :] = odd
        even, odd = alone(third)
        rows_ref[1, pl.ds(0, HALF, stride=2), :] = even
        rows_ref[1, pl.ds(1, HALF, stride=2), :] = odd
        high, rest = halves(jnp.concatenate([rows_ref[0], rows_ref[1]], axis=1))
        weights[k, 0:64, :] = high
        weights[k, 64:128, :] = high
        weights[k, 128:192, :] = rest
        weights[k, 192:256, :] = rest
        return carry

    lax.fori_loop(0, columns, weight_step, 0)

    def zero_step(i, carry):
        total[i] = jnp.zeros((BLOCK, LANES), jnp.float32)
        return carry

    lax.fori_loop(0, targets + 1, zero_step, 0)
    low_a = low_lanes(HALF)
    low = low_lanes(BLOCK)

    def multiply(c, result_ref):
        parts = []
        for u in range(CHUNK):
            value = a_ref[order_ref[c * CHUNK + u]]
            rounded = value.astype(jnp.bfloat16).astype(jnp.float32)
            rest = value - rounded
            even = jnp.where(low_a, rounded, pltpu.roll(rest, BLOCK, 1))
            odd = jnp.where(low_a, pltpu.roll(rounded, BLOCK, 1), rest)
            parts += [even.astype(jnp.bfloat16), odd.astype(jnp.bfloat16)]
        left = jnp.concatenate(parts, axis=0)
        left = jnp.concatenate([left, left], axis=1)
        result_ref[...] = jnp.dot(left, weights[chunk_ref[c]], preferred_element_type=jnp.float32)

    def add(c, result_ref):
        for u in range(CHUNK):
            at = (c + 1) * CHUNK + u
            rows = slice(u * BLOCK, (u + 1) * BLOCK)
            pair = result_ref[rows, 0:LANES]
            total[place_ref[at]] += jnp.where(low, pair, 0.0)
            total[place_ref[slots + CHUNK + at]] += jnp.where(low, 0.0, pair)
            total[place_ref[2 * (slots + CHUNK) + at]] += result_ref[rows, LANES:2 * LANES]

    second_ref[...] = jnp.zeros_like(second_ref)
    steps = (chunks_ref[0] + 1) // 2

    def chunk_step(step, carry):
        multiply(2 * step, first_ref)
        add(2 * step - 1, second_ref)
        multiply(2 * step + 1, second_ref)
        add(2 * step, first_ref)
        return carry

    lax.fori_loop(0, steps, chunk_step, 0)
    add(2 * steps - 1, second_ref)

    def out_step(i, carry):
        value = total[i]
        value = value + pltpu.roll(value, BLOCK, 1)
        out_ref[i] = jnp.where(low_a, value[0:HALF], value[HALF:BLOCK])
        return carry

    lax.fori_loop(0, targets, out_step, 0)


def coarse_kernel(rows, place_ref, ap_ref, p_ref, out_ref, result_ref):
    low = low_lanes(HALF)

    def row_step(i, carry):
        rights = []
        for pair in range(TAP // 2):
            even, odd = side_by_side(ap_ref[TAP * i + 2 * pair], ap_ref[TAP * i + 2 * pair + 1])
            rights.append(jnp.concatenate([even, odd], axis=0))
        high, rest = halves(jnp.concatenate(rights, axis=1))
        right = jnp.concatenate([high, rest, high, rest], axis=0)
        left_pair = jnp.concatenate(side_by_side(p_ref[3 * i], p_ref[3 * i + 1]), axis=0)
        left_one = jnp.concatenate(alone(p_ref[3 * i + 2]), axis=0)
        high, rest = halves(jnp.concatenate([left_pair, left_one], axis=1))
        left = jnp.concatenate([high, high, rest, rest], axis=0)
        result = lax.dot_general(
            left, right, (((0,), (0,)), ((), ())), preferred_element_type=jnp.float32
        )
        for pair in range(TAP // 2):
            result_ref[pair] = result[:, pair * LANES:(pair + 1) * LANES]
        for s in range(3):
            base = place_ref[3 * i + s] * TAP
            for pair in range(TAP // 2):
                even = result_ref[pair, pl.ds(s * BLOCK, HALF, stride=2), :]
                odd = result_ref[pair, pl.ds(s * BLOCK + 1, HALF, stride=2), :]
                out_ref[base + 2 * pair] = jnp.where(low, even, pltpu.roll(odd, BLOCK, 1))
                out_ref[base + 2 * pair + 1] = jnp.where(low, pltpu.roll(even, BLOCK, 1), odd)
        return carry

    lax.fori_loop(0, rows, row_step, 0)


def add_kernel(target_ref, in_ref, out_ref):
    out_ref[...] = jnp.zeros_like(out_ref)

    def step(e, carry):
        target = target_ref[e]

        @pl.when(target >= 0)
        def _():
            out_ref[target] += in_ref[e]

        return carry

    lax.fori_loop(0, in_ref.shape[0], step, 0)


def on_device(a_vals, a_row, a_col, a_slot, a_count, p_vals, p_owner, p_sub, ap_cslot):
    row_devices = lax.axis_size("row")
    col_devices = lax.axis_size("col")
    capacity = a_vals.shape[2]
    rows_dev = p_vals.shape[0]
    branches = p_vals.shape[1]
    group_rows = rows_dev * col_devices
    group_coarse = CPD * col_devices
    columns = rows_dev * row_devices
    targets = group_rows * TAP
    per_peer = max(2, 3 * rows_dev * branches // (2 * row_devices))
    item_count = rows_dev * branches
    slots_total = row_devices * per_peer
    f32 = jnp.float32

    p_local = p_vals.reshape(item_count, HALF, LANES)
    panel = lax.all_gather(p_local, "row", axis=0, tiled=True)

    a_blocks = a_vals.reshape(capacity, HALF, LANES)
    count = a_count.reshape(1)
    col_index = a_col.reshape(capacity)
    target = (a_row.reshape(1, capacity) * TAP + a_slot.reshape(branches, capacity)).reshape(branches * capacity)
    chunk_cap = min(capacity, columns + capacity // CHUNK) + 2
    slots = chunk_cap * CHUNK
    i32 = jnp.int32
    order, places, chunk_column, chunk_count = pl.pallas_call(
        functools.partial(plan_kernel, columns, targets),
        out_shape=(
            jax.ShapeDtypeStruct((slots,), i32),
            jax.ShapeDtypeStruct((branches * (slots + CHUNK),), i32),
            jax.ShapeDtypeStruct((chunk_cap,), i32),
            jax.ShapeDtypeStruct((1,), i32),
        ),
        in_specs=[SMEM, SMEM, SMEM],
        out_specs=(SMEM, SMEM, SMEM, SMEM),
        scratch_shapes=[pltpu.SMEM((columns,), i32)],
        cost_estimate=pl.CostEstimate(flops=0, bytes_accessed=20 << 20, transcendentals=0),
        name="plan",
    )(count, col_index, target)

    owners = p_owner.reshape(item_count)
    serial = jnp.arange(item_count, dtype=jnp.int32)
    earlier = (owners[:, None] == owners[None, :]) & (serial[None, :] < serial[:, None])
    placed = owners * per_peer + jnp.sum(earlier.astype(jnp.int32), axis=1)
    metadata = p_sub.reshape(item_count, 1) * TC + ap_cslot.reshape(item_count, TAP)
    meta_send = jnp.full((slots_total, TAP), -1.0, f32).at[placed].set(metadata.astype(f32))
    meta_in = lax.all_to_all(meta_send, "row", split_axis=0, concat_axis=0, tiled=True)
    arrived_target = meta_in.astype(jnp.int32).reshape(slots_total * TAP)

    arrived_target, chunk_count = lax.optimization_barrier((arrived_target, chunk_count))
    partial_ap = pl.pallas_call(
        functools.partial(ap_kernel, columns, targets),
        out_shape=jax.ShapeDtypeStruct((targets, HALF, LANES), f32),
        in_specs=[SMEM, SMEM, SMEM, SMEM, VMEM, VMEM],
        out_specs=VMEM,
        scratch_shapes=[
            pltpu.VMEM((columns, 4 * BLOCK, 2 * LANES), jnp.bfloat16),
            pltpu.VMEM((targets + 1, BLOCK, LANES), f32),
            pltpu.VMEM((2, BLOCK, LANES), f32),
            pltpu.VMEM((CHUNK * BLOCK, 2 * LANES), f32),
            pltpu.VMEM((CHUNK * BLOCK, 2 * LANES), f32),
        ],
        compiler_params=pltpu.CompilerParams(vmem_limit_bytes=60 << 20),
        cost_estimate=pl.CostEstimate(
            flops=capacity * 2 * 64 * 256 * 256, bytes_accessed=14 << 20, transcendentals=0
        ),
        name="ap",
    )(chunk_count, order, places, chunk_column, a_blocks, panel)

    ap_rows = lax.psum_scatter(partial_ap, "col", scatter_dimension=0, tiled=True)

    outgoing = pl.pallas_call(
        functools.partial(coarse_kernel, rows_dev),
        out_shape=jax.ShapeDtypeStruct((slots_total * TAP, HALF, LANES), f32),
        in_specs=[SMEM, VMEM, VMEM],
        out_specs=VMEM,
        scratch_shapes=[pltpu.VMEM((TAP // 2, 2 * LANES, LANES), f32)],
        compiler_params=pltpu.CompilerParams(vmem_limit_bytes=32 << 20),
        name="coarse",
    )(placed, ap_rows, p_local)

    incoming = lax.all_to_all(outgoing, "row", split_axis=0, concat_axis=0, tiled=True)

    coarse_part = pl.pallas_call(
        add_kernel,
        out_shape=jax.ShapeDtypeStruct((group_coarse * TC, HALF, LANES), f32),
        in_specs=[SMEM, VMEM],
        out_specs=VMEM,
        compiler_params=pltpu.CompilerParams(vmem_limit_bytes=32 << 20),
        name="gather_coarse",
    )(arrived_target, incoming)

    coarse = lax.psum_scatter(coarse_part, "col", scatter_dimension=0, tiled=True)
    return coarse.reshape(CPD, TC, BLOCK * BLOCK)


def solution(mesh):
    placed = (
        P("row", "col", None, None),
        P("row", "col", None),
        P("row", "col", None),
        P("row", "col", None, None),
        P("row", "col"),
        P(("row", "col"), None, None),
        P(("row", "col"), None),
        P(("row", "col"), None),
        P(("row", "col"), None, None),
    )
    return jax.shard_map(
        on_device,
        mesh=mesh,
        in_specs=placed,
        out_specs=P(("row", "col"), None, None),
        check_vma=False,
    )
```

```python
import functools

import jax
import jax.numpy as jnp
from jax import lax
from jax.experimental import pallas as pl
from jax.experimental.pallas import tpu as pltpu
from jax.sharding import PartitionSpec as P

BLOCK = 64
HALF = 32
LANES = 128
CPD = 1
TAP = 6
TC = 27
CHUNK = 4
WEIGHTS = 4
OUTS = 6

VMEM = pl.BlockSpec(memory_space=pltpu.VMEM)
SMEM = pl.BlockSpec(memory_space=pltpu.SMEM)


def low_lanes(rows):
    return lax.broadcasted_iota(jnp.int32, (rows, LANES), 1) < BLOCK


def halves(value):
    high = value.astype(jnp.bfloat16)
    return high, (value - high.astype(jnp.float32)).astype(jnp.bfloat16)


def side_by_side(first, second):
    low = low_lanes(HALF)
    even = jnp.where(low, first, pltpu.roll(second, BLOCK, 1))
    odd = jnp.where(low, pltpu.roll(first, BLOCK, 1), second)
    return even, odd


def alone(first):
    low = low_lanes(HALF)
    return jnp.where(low, first, 0.0), jnp.where(low, pltpu.roll(first, BLOCK, 1), 0.0)


def plan_kernel(columns, dump, count_ref, col_ref, target_ref, order_ref, place_ref, chunk_ref, total_ref, fill):
    capacity = col_ref.shape[0]
    slots = order_ref.shape[0]
    count = count_ref[0]

    def clear_column(k, carry):
        fill[k] = 0
        return carry

    lax.fori_loop(0, columns, clear_column, 0)

    def clear_slot(i, carry):
        order_ref[i] = 0
        for s in range(3):
            place_ref[s * (slots + CHUNK) + i] = dump
        return carry

    lax.fori_loop(0, slots, clear_slot, 0)
    for i in range(CHUNK):
        for s in range(3):
            place_ref[s * (slots + CHUNK) + slots + i] = dump

    def clear_chunk(i, carry):
        chunk_ref[i] = 0
        return carry

    lax.fori_loop(0, slots // CHUNK, clear_chunk, 0)

    def tally(t, carry):
        fill[col_ref[t]] += 1
        return carry

    lax.fori_loop(0, count, tally, 0)

    def open_column(k, first):
        chunks = (fill[k] + CHUNK - 1) // CHUNK
        fill[k] = first * CHUNK

        def mark(j, carry):
            chunk_ref[first + j] = k
            return carry

        lax.fori_loop(0, chunks, mark, 0)
        return first + chunks

    total_ref[0] = lax.fori_loop(0, columns, open_column, 0)

    def put(t, carry):
        k = col_ref[t]
        at = fill[k]
        fill[k] = at + 1
        order_ref[at] = t
        for s in range(3):
            place_ref[s * (slots + CHUNK) + CHUNK + at] = target_ref[s * capacity + t]
        return carry

    lax.fori_loop(0, count, put, 0)


def ap_kernel(columns, targets, chunks_ref, order_ref, place_ref, chunk_ref, a_ref, panel_ref, out_ref, weights, total, rows_ref, first_ref, second_ref):
    slots = order_ref.shape[0]

    def weight_step(step, carry):
        for j in range(WEIGHTS):
            k = step * WEIGHTS + j
            even, odd = side_by_side(panel_ref[3 * k], panel_ref[3 * k + 1])
            rows_ref[j, 0, pl.ds(0, HALF, stride=2), :] = even
            rows_ref[j, 0, pl.ds(1, HALF, stride=2), :] = odd
            even, odd = alone(panel_ref[3 * k + 2])
            rows_ref[j, 1, pl.ds(0, HALF, stride=2), :] = even
            rows_ref[j, 1, pl.ds(1, HALF, stride=2), :] = odd
        for j in range(WEIGHTS):
            k = step * WEIGHTS + j
            for side in range(2):
                lanes = slice(side * LANES, (side + 1) * LANES)
                high, rest = halves(rows_ref[j, side])
                weights[k, 0:64, lanes] = high
                weights[k, 64:128, lanes] = high
                weights[k, 128:192, lanes] = rest
                weights[k, 192:256, lanes] = rest
        return carry

    lax.fori_loop(0, columns // WEIGHTS, weight_step, 0)

    def zero_step(step, carry):
        for j in range(OUTS):
            total[step * OUTS + j] = jnp.zeros((BLOCK, LANES), jnp.float32)
        return carry

    lax.fori_loop(0, targets // OUTS, zero_step, 0)
    low_a = low_lanes(HALF)
    low = low_lanes(BLOCK)

    def multiply(c, result_ref):
        parts = []
        for u in range(CHUNK):
            value = a_ref[order_ref[c * CHUNK + u]]
            rounded = value.astype(jnp.bfloat16).astype(jnp.float32)
            rest = value - rounded
            even = jnp.where(low_a, rounded, pltpu.roll(rest, BLOCK, 1))
            odd = jnp.where(low_a, pltpu.roll(rounded, BLOCK, 1), rest)
            parts += [even.astype(jnp.bfloat16), odd.astype(jnp.bfloat16)]
        left = jnp.concatenate(parts, axis=0)
        left = jnp.concatenate([left, left], axis=1)
        result_ref[...] = jnp.dot(left, weights[chunk_ref[c]], preferred_element_type=jnp.float32)

    def add(c, result_ref):
        for u in range(CHUNK):
            at = (c + 1) * CHUNK + u
            rows = slice(u * BLOCK, (u + 1) * BLOCK)
            pair = result_ref[rows, 0:LANES]
            total[place_ref[at]] += jnp.where(low, pair, 0.0)
            total[place_ref[slots + CHUNK + at]] += jnp.where(low, 0.0, pair)
            total[place_ref[2 * (slots + CHUNK) + at]] += result_ref[rows, LANES:2 * LANES]

    second_ref[...] = jnp.zeros_like(second_ref)
    steps = (chunks_ref[0] + 1) // 2

    def chunk_step(step, carry):
        multiply(2 * step, first_ref)
        add(2 * step - 1, second_ref)
        multiply(2 * step + 1, second_ref)
        add(2 * step, first_ref)
        return carry

    lax.fori_loop(0, steps, chunk_step, 0)
    add(2 * steps - 1, second_ref)

    def out_step(step, carry):
        packed = []
        for j in range(OUTS):
            value = total[step * OUTS + j]
            value = value + pltpu.roll(value, BLOCK, 1)
            packed.append(jnp.where(low_a, value[0:HALF], value[HALF:BLOCK]))
        for j in range(OUTS):
            out_ref[step * OUTS + j] = packed[j]
        return carry

    lax.fori_loop(0, targets // OUTS, out_step, 0)


def coarse_kernel(rows, place_ref, ap_ref, p_ref, out_ref, result_ref):
    low = low_lanes(HALF)

    def row_step(i, carry):
        rights = []
        for pair in range(TAP // 2):
            even, odd = side_by_side(ap_ref[TAP * i + 2 * pair], ap_ref[TAP * i + 2 * pair + 1])
            rights.append(jnp.concatenate([even, odd], axis=0))
        high, rest = halves(jnp.concatenate(rights, axis=1))
        right = jnp.concatenate([high, rest, high, rest], axis=0)
        left_pair = jnp.concatenate(side_by_side(p_ref[3 * i], p_ref[3 * i + 1]), axis=0)
        left_one = jnp.concatenate(alone(p_ref[3 * i + 2]), axis=0)
        high, rest = halves(jnp.concatenate([left_pair, left_one], axis=1))
        left = jnp.concatenate([high, high, rest, rest], axis=0)
        result = lax.dot_general(
            left, right, (((0,), (0,)), ((), ())), preferred_element_type=jnp.float32
        )
        for pair in range(TAP // 2):
            result_ref[pair] = result[:, pair * LANES:(pair + 1) * LANES]
        for s in range(3):
            base = place_ref[3 * i + s] * TAP
            for pair in range(TAP // 2):
                even = result_ref[pair, pl.ds(s * BLOCK, HALF, stride=2), :]
                odd = result_ref[pair, pl.ds(s * BLOCK + 1, HALF, stride=2), :]
                out_ref[base + 2 * pair] = jnp.where(low, even, pltpu.roll(odd, BLOCK, 1))
                out_ref[base + 2 * pair + 1] = jnp.where(low, pltpu.roll(even, BLOCK, 1), odd)
        return carry

    lax.fori_loop(0, rows, row_step, 0)


def add_kernel(target_ref, in_ref, out_ref):
    out_ref[...] = jnp.zeros_like(out_ref)

    def step(e, carry):
        target = target_ref[e]

        @pl.when(target >= 0)
        def _():
            out_ref[target] += in_ref[e]

        return carry

    lax.fori_loop(0, in_ref.shape[0], step, 0)


def on_device(a_vals, a_row, a_col, a_slot, a_count, p_vals, p_owner, p_sub, ap_cslot):
    row_devices = lax.axis_size("row")
    col_devices = lax.axis_size("col")
    capacity = a_vals.shape[2]
    rows_dev = p_vals.shape[0]
    branches = p_vals.shape[1]
    group_rows = rows_dev * col_devices
    group_coarse = CPD * col_devices
    columns = rows_dev * row_devices
    targets = group_rows * TAP
    per_peer = max(2, 3 * rows_dev * branches // (2 * row_devices))
    item_count = rows_dev * branches
    slots_total = row_devices * per_peer
    f32 = jnp.float32

    p_local = p_vals.reshape(item_count, HALF, LANES)
    panel = lax.all_gather(p_local, "row", axis=0, tiled=True)

    a_blocks = a_vals.reshape(capacity, HALF, LANES)
    count = a_count.reshape(1)
    col_index = a_col.reshape(capacity)
    target = (a_row.reshape(1, capacity) * TAP + a_slot.reshape(branches, capacity)).reshape(branches * capacity)
    chunk_cap = min(capacity, columns + capacity // CHUNK) + 2
    slots = chunk_cap * CHUNK
    i32 = jnp.int32
    order, places, chunk_column, chunk_count = pl.pallas_call(
        functools.partial(plan_kernel, columns, targets),
        out_shape=(
            jax.ShapeDtypeStruct((slots,), i32),
            jax.ShapeDtypeStruct((branches * (slots + CHUNK),), i32),
            jax.ShapeDtypeStruct((chunk_cap,), i32),
            jax.ShapeDtypeStruct((1,), i32),
        ),
        in_specs=[SMEM, SMEM, SMEM],
        out_specs=(SMEM, SMEM, SMEM, SMEM),
        scratch_shapes=[pltpu.SMEM((columns,), i32)],
        cost_estimate=pl.CostEstimate(flops=0, bytes_accessed=20 << 20, transcendentals=0),
        name="plan",
    )(count, col_index, target)

    owners = p_owner.reshape(item_count)
    serial = jnp.arange(item_count, dtype=jnp.int32)
    earlier = (owners[:, None] == owners[None, :]) & (serial[None, :] < serial[:, None])
    placed = owners * per_peer + jnp.sum(earlier.astype(jnp.int32), axis=1)
    metadata = p_sub.reshape(item_count, 1) * TC + ap_cslot.reshape(item_count, TAP)
    meta_send = jnp.full((slots_total, TAP), -1.0, f32).at[placed].set(metadata.astype(f32))
    meta_in = lax.all_to_all(meta_send, "row", split_axis=0, concat_axis=0, tiled=True)
    arrived_target = meta_in.astype(jnp.int32).reshape(slots_total * TAP)

    arrived_target, chunk_count = lax.optimization_barrier((arrived_target, chunk_count))
    partial_ap = pl.pallas_call(
        functools.partial(ap_kernel, columns, targets),
        out_shape=jax.ShapeDtypeStruct((targets, HALF, LANES), f32),
        in_specs=[SMEM, SMEM, SMEM, SMEM, VMEM, VMEM],
        out_specs=VMEM,
        scratch_shapes=[
            pltpu.VMEM((columns, 4 * BLOCK, 2 * LANES), jnp.bfloat16),
            pltpu.VMEM((targets + 1, BLOCK, LANES), f32),
            pltpu.VMEM((WEIGHTS, 2, BLOCK, LANES), f32),
            pltpu.VMEM((CHUNK * BLOCK, 2 * LANES), f32),
            pltpu.VMEM((CHUNK * BLOCK, 2 * LANES), f32),
        ],
        compiler_params=pltpu.CompilerParams(vmem_limit_bytes=60 << 20),
        cost_estimate=pl.CostEstimate(
            flops=capacity * 2 * 64 * 256 * 256, bytes_accessed=14 << 20, transcendentals=0
        ),
        name="ap",
    )(chunk_count, order, places, chunk_column, a_blocks, panel)

    ap_rows = lax.psum_scatter(partial_ap, "col", scatter_dimension=0, tiled=True)

    outgoing = pl.pallas_call(
        functools.partial(coarse_kernel, rows_dev),
        out_shape=jax.ShapeDtypeStruct((slots_total * TAP, HALF, LANES), f32),
        in_specs=[SMEM, VMEM, VMEM],
        out_specs=VMEM,
        scratch_shapes=[pltpu.VMEM((TAP // 2, 2 * LANES, LANES), f32)],
        compiler_params=pltpu.CompilerParams(vmem_limit_bytes=32 << 20),
        name="coarse",
    )(placed, ap_rows, p_local)

    incoming = lax.all_to_all(outgoing, "row", split_axis=0, concat_axis=0, tiled=True)

    coarse_part = pl.pallas_call(
        add_kernel,
        out_shape=jax.ShapeDtypeStruct((group_coarse * TC, HALF, LANES), f32),
        in_specs=[SMEM, VMEM],
        out_specs=VMEM,
        compiler_params=pltpu.CompilerParams(vmem_limit_bytes=32 << 20),
        name="gather_coarse",
    )(arrived_target, incoming)

    coarse = lax.psum_scatter(coarse_part, "col", scatter_dimension=0, tiled=True)
    return coarse.reshape(CPD, TC, BLOCK * BLOCK)


def solution(mesh):
    placed = (
        P("row", "col", None, None),
        P("row", "col", None),
        P("row", "col", None),
        P("row", "col", None, None),
        P("row", "col"),
        P(("row", "col"), None, None),
        P(("row", "col"), None),
        P(("row", "col"), None),
        P(("row", "col"), None, None),
    )
    return jax.shard_map(
        on_device,
        mesh=mesh,
        in_specs=placed,
        out_specs=P(("row", "col"), None, None),
        check_vma=False,
    )
```

```python
import functools

import jax
import jax.numpy as jnp
from jax import lax
from jax.experimental import pallas as pl
from jax.experimental.pallas import tpu as pltpu
from jax.sharding import PartitionSpec as P

BLOCK = 64
HALF = 32
LANES = 128
CPD = 1
TAP = 6
TC = 27
CHUNK = 2
WEIGHTS = 4
OUTS = 6

VMEM = pl.BlockSpec(memory_space=pltpu.VMEM)
SMEM = pl.BlockSpec(memory_space=pltpu.SMEM)


def low_lanes(rows):
    return lax.broadcasted_iota(jnp.int32, (rows, LANES), 1) < BLOCK


def halves(value):
    high = value.astype(jnp.bfloat16)
    return high, (value - high.astype(jnp.float32)).astype(jnp.bfloat16)


def side_by_side(first, second):
    low = low_lanes(HALF)
    even = jnp.where(low, first, pltpu.roll(second, BLOCK, 1))
    odd = jnp.where(low, pltpu.roll(first, BLOCK, 1), second)
    return even, odd


def alone(first):
    low = low_lanes(HALF)
    return jnp.where(low, first, 0.0), jnp.where(low, pltpu.roll(first, BLOCK, 1), 0.0)


def plan_kernel(columns, dump, count_ref, col_ref, target_ref, order_ref, place_ref, chunk_ref, total_ref, fill):
    capacity = col_ref.shape[0]
    slots = order_ref.shape[0]
    count = count_ref[0]

    def clear_column(k, carry):
        fill[k] = 0
        return carry

    lax.fori_loop(0, columns, clear_column, 0)

    def clear_slot(i, carry):
        order_ref[i] = 0
        for s in range(3):
            place_ref[s * (slots + CHUNK) + i] = dump
        return carry

    lax.fori_loop(0, slots, clear_slot, 0)
    for i in range(CHUNK):
        for s in range(3):
            place_ref[s * (slots + CHUNK) + slots + i] = dump

    def clear_chunk(i, carry):
        chunk_ref[i] = 0
        return carry

    lax.fori_loop(0, slots // CHUNK, clear_chunk, 0)

    def tally(t, carry):
        fill[col_ref[t]] += 1
        return carry

    lax.fori_loop(0, count, tally, 0)

    def open_column(k, first):
        chunks = (fill[k] + CHUNK - 1) // CHUNK
        fill[k] = first * CHUNK

        def mark(j, carry):
            chunk_ref[first + j] = k
            return carry

        lax.fori_loop(0, chunks, mark, 0)
        return first + chunks

    total_ref[0] = lax.fori_loop(0, columns, open_column, 0)

    def put(t, carry):
        k = col_ref[t]
        at = fill[k]
        fill[k] = at + 1
        order_ref[at] = t
        for s in range(3):
            place_ref[s * (slots + CHUNK) + CHUNK + at] = target_ref[s * capacity + t]
        return carry

    lax.fori_loop(0, count, put, 0)


def ap_kernel(columns, targets, chunks_ref, order_ref, place_ref, chunk_ref, a_ref, panel_ref, out_ref, weights, total, rows_ref, first_ref, second_ref):
    slots = order_ref.shape[0]

    def weight_step(step, carry):
        for j in range(WEIGHTS):
            k = step * WEIGHTS + j
            even, odd = side_by_side(panel_ref[3 * k], panel_ref[3 * k + 1])
            rows_ref[j, 0, pl.ds(0, HALF, stride=2), :] = even
            rows_ref[j, 0, pl.ds(1, HALF, stride=2), :] = odd
            even, odd = alone(panel_ref[3 * k + 2])
            rows_ref[j, 1, pl.ds(0, HALF, stride=2), :] = even
            rows_ref[j, 1, pl.ds(1, HALF, stride=2), :] = odd
        for j in range(WEIGHTS):
            k = step * WEIGHTS + j
            for side in range(2):
                lanes = slice(side * LANES, (side + 1) * LANES)
                high, rest = halves(rows_ref[j, side])
                weights[k, 0:64, lanes] = high
                weights[k, 64:128, lanes] = high
                weights[k, 128:192, lanes] = rest
                weights[k, 192:256, lanes] = rest
        return carry

    lax.fori_loop(0, columns // WEIGHTS, weight_step, 0)

    def zero_step(step, carry):
        for j in range(OUTS):
            total[step * OUTS + j] = jnp.zeros((BLOCK, LANES), jnp.float32)
        return carry

    lax.fori_loop(0, targets // OUTS, zero_step, 0)
    low_a = low_lanes(HALF)
    low = low_lanes(BLOCK)

    def multiply(c, result_ref):
        parts = []
        for u in range(CHUNK):
            value = a_ref[order_ref[c * CHUNK + u]]
            rounded = value.astype(jnp.bfloat16).astype(jnp.float32)
            rest = value - rounded
            even = jnp.where(low_a, rounded, pltpu.roll(rest, BLOCK, 1))
            odd = jnp.where(low_a, pltpu.roll(rounded, BLOCK, 1), rest)
            parts += [even.astype(jnp.bfloat16), odd.astype(jnp.bfloat16)]
        left = jnp.concatenate(parts, axis=0)
        left = jnp.concatenate([left, left], axis=1)
        result_ref[...] = jnp.dot(left, weights[chunk_ref[c]], preferred_element_type=jnp.float32)

    def add(c, result_ref):
        for u in range(CHUNK):
            at = (c + 1) * CHUNK + u
            rows = slice(u * BLOCK, (u + 1) * BLOCK)
            pair = result_ref[rows, 0:LANES]
            total[place_ref[at]] += jnp.where(low, pair, 0.0)
            total[place_ref[slots + CHUNK + at]] += jnp.where(low, 0.0, pair)
            total[place_ref[2 * (slots + CHUNK) + at]] += result_ref[rows, LANES:2 * LANES]

    second_ref[...] = jnp.zeros_like(second_ref)
    steps = (chunks_ref[0] + 1) // 2

    def chunk_step(step, carry):
        multiply(2 * step, first_ref)
        add(2 * step - 1, second_ref)
        multiply(2 * step + 1, second_ref)
        add(2 * step, first_ref)
        return carry

    lax.fori_loop(0, steps, chunk_step, 0)
    add(2 * steps - 1, second_ref)

    def out_step(step, carry):
        packed = []
        for j in range(OUTS):
            value = total[step * OUTS + j]
            value = value + pltpu.roll(value, BLOCK, 1)
            packed.append(jnp.where(low_a, value[0:HALF], value[HALF:BLOCK]))
        for j in range(OUTS):
            out_ref[step * OUTS + j] = packed[j]
        return carry

    lax.fori_loop(0, targets // OUTS, out_step, 0)


def coarse_kernel(rows, place_ref, ap_ref, p_ref, out_ref, result_ref):
    low = low_lanes(HALF)

    def row_step(i, carry):
        rights = []
        for pair in range(TAP // 2):
            even, odd = side_by_side(ap_ref[TAP * i + 2 * pair], ap_ref[TAP * i + 2 * pair + 1])
            rights.append(jnp.concatenate([even, odd], axis=0))
        high, rest = halves(jnp.concatenate(rights, axis=1))
        right = jnp.concatenate([high, rest, high, rest], axis=0)
        left_pair = jnp.concatenate(side_by_side(p_ref[3 * i], p_ref[3 * i + 1]), axis=0)
        left_one = jnp.concatenate(alone(p_ref[3 * i + 2]), axis=0)
        high, rest = halves(jnp.concatenate([left_pair, left_one], axis=1))
        left = jnp.concatenate([high, high, rest, rest], axis=0)
        result = lax.dot_general(
            left, right, (((0,), (0,)), ((), ())), preferred_element_type=jnp.float32
        )
        for pair in range(TAP // 2):
            result_ref[pair] = result[:, pair * LANES:(pair + 1) * LANES]
        for s in range(3):
            base = place_ref[3 * i + s] * TAP
            for pair in range(TAP // 2):
                even = result_ref[pair, pl.ds(s * BLOCK, HALF, stride=2), :]
                odd = result_ref[pair, pl.ds(s * BLOCK + 1, HALF, stride=2), :]
                out_ref[base + 2 * pair] = jnp.where(low, even, pltpu.roll(odd, BLOCK, 1))
                out_ref[base + 2 * pair + 1] = jnp.where(low, pltpu.roll(even, BLOCK, 1), odd)
        return carry

    lax.fori_loop(0, rows, row_step, 0)


def add_kernel(target_ref, in_ref, out_ref):
    out_ref[...] = jnp.zeros_like(out_ref)

    def step(e, carry):
        target = target_ref[e]

        @pl.when(target >= 0)
        def _():
            out_ref[target] += in_ref[e]

        return carry

    lax.fori_loop(0, in_ref.shape[0], step, 0)


def on_device(a_vals, a_row, a_col, a_slot, a_count, p_vals, p_owner, p_sub, ap_cslot):
    row_devices = lax.axis_size("row")
    col_devices = lax.axis_size("col")
    capacity = a_vals.shape[2]
    rows_dev = p_vals.shape[0]
    branches = p_vals.shape[1]
    group_rows = rows_dev * col_devices
    group_coarse = CPD * col_devices
    columns = rows_dev * row_devices
    targets = group_rows * TAP
    per_peer = max(2, 3 * rows_dev * branches // (2 * row_devices))
    item_count = rows_dev * branches
    slots_total = row_devices * per_peer
    f32 = jnp.float32

    p_local = p_vals.reshape(item_count, HALF, LANES)
    panel = lax.all_gather(p_local, "row", axis=0, tiled=True)

    a_blocks = a_vals.reshape(capacity, HALF, LANES)
    count = a_count.reshape(1)
    col_index = a_col.reshape(capacity)
    target = (a_row.reshape(1, capacity) * TAP + a_slot.reshape(branches, capacity)).reshape(branches * capacity)
    chunk_cap = min(capacity, columns + capacity // CHUNK) + 2
    slots = chunk_cap * CHUNK
    i32 = jnp.int32
    order, places, chunk_column, chunk_count = pl.pallas_call(
        functools.partial(plan_kernel, columns, targets),
        out_shape=(
            jax.ShapeDtypeStruct((slots,), i32),
            jax.ShapeDtypeStruct((branches * (slots + CHUNK),), i32),
            jax.ShapeDtypeStruct((chunk_cap,), i32),
            jax.ShapeDtypeStruct((1,), i32),
        ),
        in_specs=[SMEM, SMEM, SMEM],
        out_specs=(SMEM, SMEM, SMEM, SMEM),
        scratch_shapes=[pltpu.SMEM((columns,), i32)],
        cost_estimate=pl.CostEstimate(flops=0, bytes_accessed=20 << 20, transcendentals=0),
        name="plan",
    )(count, col_index, target)

    owners = p_owner.reshape(item_count)
    serial = jnp.arange(item_count, dtype=jnp.int32)
    earlier = (owners[:, None] == owners[None, :]) & (serial[None, :] < serial[:, None])
    placed = owners * per_peer + jnp.sum(earlier.astype(jnp.int32), axis=1)
    metadata = p_sub.reshape(item_count, 1) * TC + ap_cslot.reshape(item_count, TAP)
    meta_send = jnp.full((slots_total, TAP), -1.0, f32).at[placed].set(metadata.astype(f32))
    meta_in = lax.all_to_all(meta_send, "row", split_axis=0, concat_axis=0, tiled=True)
    arrived_target = meta_in.astype(jnp.int32).reshape(slots_total * TAP)

    arrived_target, chunk_count = lax.optimization_barrier((arrived_target, chunk_count))
    partial_ap = pl.pallas_call(
        functools.partial(ap_kernel, columns, targets),
        out_shape=jax.ShapeDtypeStruct((targets, HALF, LANES), f32),
        in_specs=[SMEM, SMEM, SMEM, SMEM, VMEM, VMEM],
        out_specs=VMEM,
        scratch_shapes=[
            pltpu.VMEM((columns, 4 * BLOCK, 2 * LANES), jnp.bfloat16),
            pltpu.VMEM((targets + 1, BLOCK, LANES), f32),
            pltpu.VMEM((WEIGHTS, 2, BLOCK, LANES), f32),
            pltpu.VMEM((CHUNK * BLOCK, 2 * LANES), f32),
            pltpu.VMEM((CHUNK * BLOCK, 2 * LANES), f32),
        ],
        compiler_params=pltpu.CompilerParams(vmem_limit_bytes=60 << 20),
        cost_estimate=pl.CostEstimate(
            flops=capacity * 2 * 64 * 256 * 256, bytes_accessed=14 << 20, transcendentals=0
        ),
        name="ap",
    )(chunk_count, order, places, chunk_column, a_blocks, panel)

    ap_rows = lax.psum_scatter(partial_ap, "col", scatter_dimension=0, tiled=True)

    outgoing = pl.pallas_call(
        functools.partial(coarse_kernel, rows_dev),
        out_shape=jax.ShapeDtypeStruct((slots_total * TAP, HALF, LANES), f32),
        in_specs=[SMEM, VMEM, VMEM],
        out_specs=VMEM,
        scratch_shapes=[pltpu.VMEM((TAP // 2, 2 * LANES, LANES), f32)],
        compiler_params=pltpu.CompilerParams(vmem_limit_bytes=32 << 20),
        name="coarse",
    )(placed, ap_rows, p_local)

    incoming = lax.all_to_all(outgoing, "row", split_axis=0, concat_axis=0, tiled=True)

    coarse_part = pl.pallas_call(
        add_kernel,
        out_shape=jax.ShapeDtypeStruct((group_coarse * TC, HALF, LANES), f32),
        in_specs=[SMEM, VMEM],
        out_specs=VMEM,
        compiler_params=pltpu.CompilerParams(vmem_limit_bytes=32 << 20),
        name="gather_coarse",
    )(arrived_target, incoming)

    coarse = lax.psum_scatter(coarse_part, "col", scatter_dimension=0, tiled=True)
    return coarse.reshape(CPD, TC, BLOCK * BLOCK)


def solution(mesh):
    placed = (
        P("row", "col", None, None),
        P("row", "col", None),
        P("row", "col", None),
        P("row", "col", None, None),
        P("row", "col"),
        P(("row", "col"), None, None),
        P(("row", "col"), None),
        P(("row", "col"), None),
        P(("row", "col"), None, None),
    )
    return jax.shard_map(
        on_device,
        mesh=mesh,
        in_specs=placed,
        out_specs=P(("row", "col"), None, None),
        check_vma=False,
    )
```
